256 devices in a mesh: vp: 64 (over y_hi, z, x), ch: 4 (over y_lo, core).
Axes of the slice: x: 4, y: 4 (y_hi: 2, y_lo: 2; y = y_hi * 2 + y_lo), z: 8, core: 2. Of those that a mesh axis runs over, the one named last changes fastest.
Arguments:
- chol_a: bfloat16 [640, 4, 6000], P('vp', None, 'ch'), may hold values from -0.078125 to 0.078125
- chol_b: bfloat16 [6000, 64, 640], P('ch', 'vp'), may hold values from -6 to 6
- amplitudes: bfloat16 [640, 8, 640], P('vp'), may hold values from -0.0390625 to 0.0390625
- vir_a: float32 [4], replicated, may hold values from 0.2 to 3
- vir_b: float32 [64], P('vp'), may hold values from 0.2 to 3
- occ_pair: float32 [8], P('ch'), may hold values from -4 to -1
Outputs:
- increment: float32 [4, 64, 8], P(None, 'vp', 'ch')
The draws below stay inside these ranges and needn't reach their ends.
All inputs are finite; a program needn't handle non-finite values.
Results may differ from the reference program's by a relative error of at most 0.0029.
Values may be sent and summed in bfloat16 or wider, within the bound.
A program may use at most 64 MiB of HBM per device.

```python
import jax
import jax.numpy as jnp
from jax import lax

NV = 640
NCH = 6000
NIJ = 8
NA = 4
NB = 64
N_CH = 4


def block_levels(key, dims, cuts, smallest, top_value):
    gain = 1.0
    for position, blocks in cuts:
        draws = jax.random.uniform(jax.random.fold_in(jax.random.fold_in(key, 6), position), (blocks,), jnp.float32, smallest / len(cuts), top_value / len(cuts))
        gain = gain * jnp.repeat(jnp.exp(draws), dims[position] // blocks).reshape((-1,) + (1,) * (len(dims) - 1 - position))
    return gain


def gaussian(own_key, extent, deviation, bound, pieces=(), kind=jnp.bfloat16):
    drawn = deviation * jax.random.normal(own_key, extent, jnp.float32)
    if pieces:
        drawn = drawn * block_levels(own_key, extent, pieces, -0.22, 0.18)
    return jnp.clip(drawn, -bound, bound).astype(kind)


def setup_inputs(seed: int = 0) -> dict:
    seeds = jax.random.split(jax.random.key(seed), 7)
    chol_a = gaussian(seeds[0], (NV, NA, NCH), NCH ** -0.5, 0.078125, ((0, 64), (2, 4)))
    chol_b = gaussian(seeds[1], (NCH, NB, NV), 1.0, 6.0, ((0, 4), (1, 64)))
    amplitudes = gaussian(seeds[2], (NV, NIJ, NV), (NV * NV // 16) ** -0.5, 0.0390625, ((0, 64),))
    vir_a = jnp.clip(jax.random.uniform(seeds[3], (NA,), jnp.float32, 0.2, 3.0), 0.2, 3.0)
    vir_b = jnp.clip(0.2 + 2.8 * jax.random.uniform(seeds[4], (NB,), jnp.float32) ** block_levels(seeds[4], (NB,), ((0, 64),), -0.2, 0.2), 0.2, 3.0)
    occ_pair = jnp.clip(-4.0 + 3.0 * jax.random.uniform(seeds[5], (NIJ,), jnp.float32) ** block_levels(seeds[5], (NIJ,), ((0, 4),), -0.2, 0.2), -4.0, -1.0)
    return {"chol_a": chol_a, "chol_b": chol_b, "amplitudes": amplitudes, "vir_a": vir_a, "vir_b": vir_b, "occ_pair": occ_pair}


def reference(chol_a, chol_b, amplitudes, vir_a, vir_b, occ_pair):
    slab_width = NCH // N_CH
    left_all = chol_a.reshape(NV * NA, NCH)
    amps_f32 = amplitudes.astype(jnp.float32)

    def ladder_row(b_index):
        running = jnp.zeros((NA, NIJ), jnp.float32)
        for slab_id in range(N_CH):
            left = left_all[:, slab_id * slab_width:(slab_id + 1) * slab_width]
            cholesky_right = lax.dynamic_slice_in_dim(chol_b[slab_id * slab_width:(slab_id + 1) * slab_width], b_index, 1, 1).reshape(slab_width, NV)
            v_rows = jnp.dot(left, cholesky_right, preferred_element_type=jnp.float32).astype(jnp.bfloat16)
            v_rows = lax.optimization_barrier(v_rows).astype(jnp.float32).reshape(NV, NA, NV)
            running = running + jnp.einsum('cad,cid->ai', v_rows, amps_f32, precision=lax.Precision.HIGHEST)
        return running

    ladder = lax.map(ladder_row, jnp.arange(NB, dtype=jnp.int32))
    ladder = jnp.transpose(ladder, (1, 0, 2))
    energy_gap = vir_a[:, None, None] + vir_b[None, :, None] - occ_pair[None, None, :]
    return ladder / energy_gap
```

```python
import functools

import jax
import jax.numpy as jnp
from jax import lax
from jax.experimental import pallas as pl
from jax.experimental.pallas import tpu as pltpu
from jax.sharding import PartitionSpec as P

MESH = pl.DeviceIdType.MESH
NX, NZ = 4, 8
PQ = 384
BF16, F32 = jnp.bfloat16, jnp.float32


def kernel(a_in, b_in, t_in, out, a_stage, a_buf, t_buf, b_buf, hl, g_acc, r_send, r_in,
           a_ssem, a_rsem, t_ssem, t_rsem, b_ssem, b_rsem, f_ssem, f_rsem,
           za_ssem, za_rsem, zt_ssem, zt_rsem, y_ssem, y_rsem, r_ssem, r_rsem, l_sem):
    vp, ch = lax.axis_index("vp"), lax.axis_index("ch")
    x, z, h = vp % NX, (vp // NX) % NZ, vp // (NX * NZ)
    k, l = ch % 2, ch // 2

    def dev(x_, z_, h_, l_, k_):
        return (h_ * (NX * NZ) + z_ * NX + x_, l_ * 2 + k_)

    def remote(src, dst, ssem, rsem, device):
        return pltpu.make_async_remote_copy(
            src_ref=src, dst_ref=dst, send_sem=ssem, recv_sem=rsem, device_id=device, device_id_type=MESH)

    sibling = dev(x, z, h, l, 1 - k)
    up, down = (z + 1) % NZ, (z + NZ - 1) % NZ
    above, below = dev(x, up, h, l, k), dev(x, down, h, l, k)
    across = dev(x, z, 1 - h, 1 - l, h)
    mine = k == h

    barrier = pltpu.get_barrier_semaphore()
    q32 = x * 8 + h * 4 + l * 2 + k

    def greet(i, carry):
        q = (q32 + i) % 32
        pl.semaphore_signal(barrier, inc=1, device_id=dev(q // 8, z, (q // 4) % 2, (q // 2) % 2, q % 2),
                            device_id_type=MESH)
        return carry

    lax.fori_loop(1, 32, greet, 0)
    pl.semaphore_signal(barrier, inc=1, device_id=above, device_id_type=MESH)
    pl.semaphore_signal(barrier, inc=1, device_id=below, device_id_type=MESH)
    pl.semaphore_wait(barrier, 33)

    slot = 2 * x + k
    a_copies = []
    for dh in range(2):
        for dx in range(NX):
            to_x, to_h = (x + dx) % NX, (h + dh) % 2
            copy = remote(a_in.at[to_x], a_stage.at[slot], a_ssem.at[dh * NX + dx], a_rsem.at[slot],
                          dev(to_x, z, to_h, l, h))
            if dh == 0 and dx == 0:
                @pl.when(mine)
                def _():
                    pltpu.make_async_copy(a_in.at[x], a_stage.at[slot], a_rsem.at[slot]).start()

                @pl.when(jnp.logical_not(mine))
                def _():
                    copy.start()
            else:
                copy.start()
            a_copies.append(copy)

    t_own = pl.ds(pl.multiple_of(80 * x, 16), 80)
    t_copies = []
    for dx in range(1, NX):
        t_copies.append(remote(t_in, t_buf.at[z, t_own], t_ssem.at[dx], t_rsem.at[dx], dev((x + dx) % NX, z, h, l, k)))
    t_local = pltpu.make_async_copy(t_in, t_buf.at[z, t_own], l_sem.at[0])

    @pl.when(mine)
    def _():
        for copy in t_copies:
            copy.start()
        t_local.start()

    def b_rows(core):
        return pl.ds(pl.multiple_of(core * PQ, PQ), PQ)

    def b_quarter(q):
        return pl.ds(pl.multiple_of(q * PQ, PQ), PQ)

    b_copies = {}
    for dx in (1, 3, 2):
        to_x = (x + dx) % NX
        b_copies[dx] = remote(b_in.at[b_quarter(to_x)], b_buf.at[x, b_rows(k)], b_ssem.at[dx], b_rsem.at[dx],
                              dev(to_x, z, h, l, k))
        b_copies[dx].start()
    b_local = pltpu.make_async_copy(b_in.at[b_quarter(x)], b_buf.at[x, b_rows(k)], l_sem.at[1])
    b_local.start()
    f_copies = {0: remote(b_in.at[b_quarter(x)], b_buf.at[x, b_rows(k)], f_ssem.at[0], f_rsem.at[0], sibling)}
    f_copies[0].start()

    def ring(buf, ssem, rsem, half, step):
        lo_block, hi_block = (z + NZ - step) % NZ, (z + step) % NZ
        if step < 3:
            lo_ref, hi_ref = buf.at[lo_block], buf.at[hi_block]
        else:
            lo_ref, hi_ref = buf.at[lo_block, pl.ds(0, half)], buf.at[hi_block, pl.ds(half, half)]
        return (remote(lo_ref, lo_ref, ssem.at[2 * step], rsem.at[2 * step], above),
                remote(hi_ref, hi_ref, ssem.at[2 * step + 1], rsem.at[2 * step + 1], below))

    def arrived(buf, ssem, rsem, half, step):
        lo_block, hi_block = (z + NZ - 1 - step) % NZ, (z + 1 + step) % NZ
        if step < 3:
            lo_ref, hi_ref = buf.at[lo_block], buf.at[hi_block]
        else:
            lo_ref, hi_ref = buf.at[lo_block, pl.ds(0, half)], buf.at[hi_block, pl.ds(half, half)]
        remote(lo_ref, lo_ref, ssem.at[2 * step], rsem.at[2 * step], below).wait_recv()
        remote(hi_ref, hi_ref, ssem.at[2 * step + 1], rsem.at[2 * step + 1], above).wait_recv()

    za = functools.partial(ring, a_buf, za_ssem, za_rsem, 80)
    zt = functools.partial(ring, t_buf, zt_ssem, zt_rsem, 160)

    def y_copy(offset):
        block = (z + offset) % NZ
        return remote(t_buf.at[block], t_buf.at[block], y_ssem.at[offset], y_rsem.at[offset], across)

    for origin in range(2 * NX):
        remote(a_stage.at[origin], a_stage.at[origin], a_ssem.at[0], a_rsem.at[origin], sibling).wait_recv()
    for part in range(2):
        rows = [a_stage[2 * origin + part].astype(F32) for origin in range(NX)]
        a_buf[z, :, part * PQ:(part + 1) * PQ] = jnp.concatenate(rows, axis=0).astype(BF16)
    for copy in za(0):
        copy.start()

    @pl.when(mine)
    def _():
        for dx in range(1, NX):
            origin = pl.ds(pl.multiple_of(80 * ((x + NX - dx) % NX), 16), 80)
            remote(t_buf.at[z, origin], t_buf.at[z, origin], t_ssem.at[dx], t_rsem.at[dx], sibling).wait_recv()
        t_local.wait()
        for copy in zt(0):
            copy.start()
        y_copy(0).start()

    g_acc[...] = jnp.zeros_like(g_acc)

    def advance(step):
        arrived(a_buf, za_ssem, za_rsem, 80, step)
        if step < 3:
            for copy in za(step + 1):
                copy.start()

        @pl.when(mine)
        def _():
            arrived(t_buf, zt_ssem, zt_rsem, 160, step)
            if step < 3:
                for copy in zt(step + 1):
                    copy.start()
            for offset in ((1 + step, 7 - step) if step < 3 else (4,)):
                y_copy(offset).start()

    def t_here(*offsets):
        @pl.when(jnp.logical_not(mine))
        def _():
            for offset in offsets:
                y_copy(offset).wait_recv()

    def b_arrived(dx):
        origin = (x + NX - dx) % NX
        ref = b_buf.at[origin, b_rows(k)]
        remote(ref, ref, b_ssem.at[dx], b_rsem.at[dx], sibling).wait_recv()
        f_copies[dx] = remote(ref, ref, f_ssem.at[dx], f_rsem.at[dx], sibling)
        f_copies[dx].start()

    def compute(first, second):
        blocks = ((z + first) % NZ, (z + second) % NZ)

        def product(b, carry):
            left = jnp.concatenate([a_buf[blocks[0]], a_buf[blocks[1]]], axis=0)
            v = jnp.dot(left, b_buf[b], preferred_element_type=F32)
            high = v.astype(BF16)
            low = (v - high.astype(F32)).astype(BF16)
            for j in range(4):
                hl[j, pl.ds(pl.multiple_of(b * 160, 16), 80)] = high[80 * j:80 * j + 80]
                hl[j, pl.ds(pl.multiple_of(b * 160 + 80, 16), 80)] = low[80 * j:80 * j + 80]
            return carry

        lax.fori_loop(0, NX, product, 0)
        for j in range(4):
            g_acc[...] += lax.dot_general(
                hl[j], t_buf[blocks[j // 2], 160 * (j % 2):160 * (j % 2) + 160],
                (((1,), (1,)), ((), ())), preferred_element_type=F32)

    advance(0)
    b_arrived(1)
    b_arrived(3)
    advance(1)
    b_arrived(2)
    b_local.wait()
    for dx in range(NX):
        ref = b_buf.at[(x + NX - dx) % NX, b_rows(1 - k)]
        remote(ref, ref, f_ssem.at[dx], f_rsem.at[dx], sibling).wait_recv()
    t_here(0, 1)
    compute(0, 1)
    advance(2)
    t_here(7, 2)
    compute(7, 2)
    t_here(6, 3)
    compute(6, 3)
    advance(3)
    t_here(5, 4)
    compute(5, 4)

    row = lax.broadcasted_iota(jnp.int32, (80, 160), 0)
    col = lax.broadcasted_iota(jnp.int32, (80, 160), 1)
    diagonal = (row // 4) == (col // 8)
    left = ((lax.broadcasted_iota(jnp.int32, (8, 80), 1) % 4) == lax.broadcasted_iota(jnp.int32, (8, 80), 0)).astype(F32)
    right = ((lax.broadcasted_iota(jnp.int32, (160, 128), 0) % 8)
             == lax.broadcasted_iota(jnp.int32, (160, 128), 1)).astype(F32)
    for b in range(NX):
        both = g_acc[160 * b:160 * b + 80] + g_acc[160 * b + 80:160 * b + 160]
        both = jnp.where(diagonal, both, 0.0)
        half = jnp.dot(left, both, precision=lax.Precision.HIGHEST, preferred_element_type=F32)
        r_send[b] = jnp.dot(half, right, precision=lax.Precision.HIGHEST, preferred_element_type=F32)

    q16 = x * 4 + l * 2 + k
    r_copies = []
    for d in range(1, 16):
        q = (q16 + d) % 16
        copy = remote(r_send.at[q // 4], r_in.at[d], r_ssem.at[d], r_rsem.at[d],
                      dev(q // 4, z, h, (q // 2) % 2, q % 2))
        copy.start()
        r_copies.append(copy)
    total = r_send[x]
    for d, copy in enumerate(r_copies, 1):
        copy.wait_recv()
        total = total + r_in[d]
    out[...] = total

    for copy in r_copies:
        copy.wait_send()
    for i, copy in enumerate(a_copies):
        if i == 0:
            @pl.when(jnp.logical_not(mine))
            def _():
                copy.wait_send()
        else:
            copy.wait_send()
    for dx in (1, 2, 3):
        b_copies[dx].wait_send()
    for dx in range(NX):
        f_copies[dx].wait_send()
    for step in range(4):
        for copy in za(step):
            copy.wait_send()

    @pl.when(mine)
    def _():
        for copy in t_copies:
            copy.wait_send()
        for step in range(4):
            for copy in zt(step):
                copy.wait_send()
        for offset in range(NZ):
            y_copy(offset).wait_send()


def body(chol_a, chol_b, amplitudes, vir_a, vir_b, occ_pair):
    a_in = jnp.pad(chol_a.reshape(40, 1500), ((0, 0), (0, NX * PQ - 1500)))
    a_in = a_in.reshape(40, NX, PQ).transpose(1, 0, 2)
    b_in = jnp.pad(chol_b.reshape(1500, 640), ((0, NX * PQ - 1500), (0, 0)))
    t_in = amplitudes.reshape(80, 640)
    dma = pltpu.SemaphoreType.DMA
    tile = pl.pallas_call(
        kernel,
        out_shape=jax.ShapeDtypeStruct((8, 128), F32),
        in_specs=[pl.BlockSpec(memory_space=pltpu.VMEM), pl.BlockSpec(memory_space=pl.ANY),
                  pl.BlockSpec(memory_space=pltpu.VMEM)],
        out_specs=pl.BlockSpec(memory_space=pltpu.VMEM),
        scratch_shapes=[
            pltpu.VMEM((2 * NX, 40, PQ), BF16),
            pltpu.VMEM((NZ, 160, 2 * PQ), BF16),
            pltpu.VMEM((NZ, 320, 640), BF16),
            pltpu.VMEM((NX, 2 * PQ, 640), BF16),
            pltpu.VMEM((4, 640, 640), BF16),
            pltpu.VMEM((640, 160), F32),
            pltpu.VMEM((NX, 8, 128), F32),
            pltpu.VMEM((16, 8, 128), F32),
            dma((8,)), dma((8,)), dma((4,)), dma((4,)), dma((4,)), dma((4,)), dma((4,)), dma((4,)),
            dma((8,)), dma((8,)), dma((8,)), dma((8,)), dma((8,)), dma((8,)), dma((16,)), dma((16,)), dma((2,)),
        ],
        compiler_params=pltpu.CompilerParams(
            collective_id=0, has_side_effects=True, vmem_limit_bytes=48 * 1024 * 1024),
        cost_estimate=pl.CostEstimate(flops=7_000_000_000, bytes_accessed=16_000_000, transcendentals=0),
    )(a_in, b_in, t_in)
    pairs = occ_pair.shape[0]
    ladder = lax.dynamic_slice_in_dim(tile[:4], lax.axis_index("ch") * pairs, pairs, 1)
    energy_gap = vir_a[:, None, None] + vir_b[None, :, None] - occ_pair[None, None, :]
    return ladder[:, None, :] / energy_gap


def solution(mesh):
    return jax.shard_map(
        body,
        mesh=mesh,
        in_specs=(
            P("vp", None, "ch"),
            P("ch", "vp", None),
            P("vp", None, None),
            P(),
            P("vp"),
            P("ch"),
        ),
        out_specs=P(None, "vp", "ch"),
        check_vma=False,
    )
```

```python
import functools

import jax
import jax.numpy as jnp
from jax import lax
from jax.experimental import pallas as pl
from jax.experimental.pallas import tpu as pltpu
from jax.sharding import PartitionSpec as P

MESH = pl.DeviceIdType.MESH
NX, NZ = 4, 8
PQ = 384
SLOTS = (0, 1, 3, 2)
BF16, F32 = jnp.bfloat16, jnp.float32


def kernel(a_in, b_in, t_in, out, a_stage, a_buf, t_buf, b_buf, hl, g_acc, r_send, r_in,
           a_ssem, a_rsem, t_ssem, t_rsem, b_ssem, b_rsem, f_ssem, f_rsem,
           za_ssem, za_rsem, zt_ssem, zt_rsem, p_ssem, p_rsem, c_ssem, c_rsem, d_ssem, d_rsem,
           r_ssem, r_rsem, l_sem):
    vp, ch = lax.axis_index("vp"), lax.axis_index("ch")
    x, z, h = vp % NX, (vp // NX) % NZ, vp // (NX * NZ)
    k, l = ch % 2, ch // 2

    def dev(x_, z_, h_, l_, k_):
        return (h_ * (NX * NZ) + z_ * NX + x_, l_ * 2 + k_)

    def remote(src, dst, ssem, rsem, device):
        return pltpu.make_async_remote_copy(
            src_ref=src, dst_ref=dst, send_sem=ssem, recv_sem=rsem, device_id=device, device_id_type=MESH)

    def rows(start, size):
        return pl.ds(pl.multiple_of(start, 16), size)

    sibling = dev(x, z, h, l, 1 - k)
    above, below = dev(x, (z + 1) % NZ, h, l, k), dev(x, (z + NZ - 1) % NZ, h, l, k)
    pair = dev(x, z, h, 1 - l, k)
    across = dev(x, z, 1 - h, 1 - l, k)
    mine = k == h
    other = jnp.logical_not(mine)

    barrier = pltpu.get_barrier_semaphore()
    q32 = x * 8 + h * 4 + l * 2 + k

    def greet(i, carry):
        q = (q32 + i) % 32
        pl.semaphore_signal(barrier, inc=1, device_id=dev(q // 8, z, (q // 4) % 2, (q // 2) % 2, q % 2),
                            device_id_type=MESH)
        return carry

    lax.fori_loop(1, 32, greet, 0)
    pl.semaphore_signal(barrier, inc=1, device_id=above, device_id_type=MESH)
    pl.semaphore_signal(barrier, inc=1, device_id=below, device_id_type=MESH)
    pl.semaphore_wait(barrier, 33)

    slot = 2 * x + k
    a_copies = []
    for dh in range(2):
        for dx in range(NX):
            to_x, to_h = (x + dx) % NX, (h + dh) % 2
            copy = remote(a_in.at[to_x], a_stage.at[slot], a_ssem.at[dh * NX + dx], a_rsem.at[slot],
                          dev(to_x, z, to_h, l, h))
            if dh == 0 and dx == 0:
                @pl.when(mine)
                def _():
                    pltpu.make_async_copy(a_in.at[x], a_stage.at[slot], a_rsem.at[slot]).start()

                @pl.when(other)
                def _():
                    copy.start()
            else:
                copy.start()
            a_copies.append(copy)

    t_copies = [remote(t_in, t_buf.at[z, rows(80 * x, 80)], t_ssem.at[dx], t_rsem.at[x % 2],
                       dev((x + dx) % NX, z, h, l, k)) for dx in range(1, NX)]
    t_local = pltpu.make_async_copy(t_in, t_buf.at[z, rows(80 * x, 80)], t_rsem.at[x % 2])
    t_mine = jnp.logical_and(mine, x // 2 == l)

    @pl.when(t_mine)
    def _():
        for copy in t_copies:
            copy.start()
        t_local.start()

    def b_rows(core):
        return rows(core * PQ, PQ)

    def b_copy(s):
        to_x = (x + SLOTS[s]) % NX
        return remote(b_in.at[rows(to_x * PQ, PQ)], b_buf.at[s, b_rows(k)], b_ssem.at[s], b_rsem.at[s],
                      dev(to_x, z, h, l, k))

    def f_copy(s):
        src = b_in.at[rows(x * PQ, PQ)] if s == 0 else b_buf.at[s, b_rows(k)]
        return remote(src, b_buf.at[s, b_rows(k)], f_ssem.at[s], f_rsem.at[s], sibling)

    for s in range(1, NX):
        b_copy(s).start()
    b_local = pltpu.make_async_copy(b_in.at[rows(x * PQ, PQ)], b_buf.at[0, b_rows(k)], l_sem.at[0])
    b_local.start()
    f_copy(0).start()

    def last(way, half):
        return 3 if way == half else 2

    def block_of(offset):
        return (z + offset) % NZ

    def za(way, half, step, offset):
        ref = a_buf.at[block_of(offset), pl.ds(80 * half, 80)]
        i = (way * 2 + half) * 4 + step
        return remote(ref, ref, za_ssem.at[i], za_rsem.at[i], above if way == 0 else below)

    def zt(way, half, step, offset):
        ref = t_buf.at[block_of(offset), rows(160 * l + 80 * half, 80)]
        i = (way * 2 + half) * 4 + step
        return remote(ref, ref, zt_ssem.at[i], zt_rsem.at[i], above if way == 0 else below)

    def sent_offset(way, step):
        return (NZ - step) % NZ if way == 0 else step

    def got_offset(way, step):
        return NZ - 1 - step if way == 0 else 1 + step

    def unit(offset, which):
        return t_buf.at[block_of(offset), rows(160 * which, 160)]

    def quarter(offset, which, part):
        return t_buf.at[block_of(offset), rows(160 * which + 80 * part, 80)]

    def to_pair(offset, which):
        return remote(unit(offset, which), unit(offset, which), p_ssem.at[offset], p_rsem.at[offset], pair)

    def to_across(offset, which):
        return remote(unit(offset, which), unit(offset, which), c_ssem.at[offset], c_rsem.at[offset], across)

    def more_across(offset, which):
        ref = quarter(offset, which, 1)
        return remote(ref, ref, d_ssem.at[offset], d_rsem.at[offset], across)

    def more_pair(offset, which):
        ref = quarter(offset, which, 0)
        return remote(ref, ref, p_ssem.at[offset], p_rsem.at[offset], pair)

    for origin in range(2 * NX):
        remote(a_stage.at[origin], a_stage.at[origin], a_ssem.at[0], a_rsem.at[origin], sibling).wait_recv()
    for part in range(2):
        pieces = [a_stage[2 * origin + part].astype(F32) for origin in range(NX)]
        a_buf[z, :, part * PQ:(part + 1) * PQ] = jnp.concatenate(pieces, axis=0).astype(BF16)
    for half in range(2):
        for way in range(2):
            za(way, half, 0, 0).start()

    @pl.when(mine)
    def _():
        for half in range(2):
            ref = quarter(0, l, half)
            remote(ref, ref, t_ssem.at[0], t_rsem.at[half], sibling).wait_recv()
            for way in range(2):
                zt(way, half, 0, 0).start()
        to_pair(0, l).start()
        to_across(0, l).start()

    g_acc[...] = jnp.zeros_like(g_acc)

    def arrive(step):
        for half in range(2):
            ways = [way for way in range(2) if step <= last(way, half)]
            for way in ways:
                offset = got_offset(way, step)
                za(way, half, step, offset).wait_recv()
                if step < last(way, half):
                    za(way, half, step + 1, offset).start()

            @pl.when(mine)
            def _():
                for way in ways:
                    offset = got_offset(way, step)
                    zt(way, half, step, offset).wait_recv()
                    if step < last(way, half):
                        zt(way, half, step + 1, offset).start()

        @pl.when(mine)
        def _():
            for offset in ((7 - step, 1 + step) if step < 3 else (4,)):
                to_pair(offset, l).start()
                to_across(offset, l).start()

    def relay(*offsets):
        @pl.when(mine)
        def _():
            for offset in offsets:
                to_pair(offset, 1 - l).wait_recv()
                more_across(offset, 1 - l).start()

        @pl.when(other)
        def _():
            for offset in offsets:
                to_across(offset, 1 - l).wait_recv()
                more_pair(offset, 1 - l).start()

    def complete(*offsets):
        @pl.when(other)
        def _():
            for offset in offsets:
                more_across(offset, l).wait_recv()
                more_pair(offset, l).wait_recv()

    def b_arrived(s):
        ref = b_buf.at[s, b_rows(k)]
        remote(ref, ref, b_ssem.at[s], b_rsem.at[s], sibling).wait_recv()
        f_copy(s).start()

    def b_complete(s):
        if s == 0:
            b_local.wait()
        ref = b_buf.at[s, b_rows(1 - k)]
        remote(ref, ref, f_ssem.at[s], f_rsem.at[s], sibling).wait_recv()

    groups = ((0, 1), (7, 2), (6, 3), (5, 4))

    def product(g, first, end):
        blocks = [block_of(offset) for offset in groups[g]]

        def one(b, carry):
            left = jnp.concatenate([a_buf[blocks[0]], a_buf[blocks[1]]], axis=0)
            v = jnp.dot(left, b_buf[b], preferred_element_type=F32)
            high = v.astype(BF16)
            low = (v - high.astype(F32)).astype(BF16)
            for j in range(4):
                hl[4 * g + j, rows(b * 160, 80)] = high[80 * j:80 * j + 80]
                hl[4 * g + j, rows(b * 160 + 80, 80)] = low[80 * j:80 * j + 80]
            return carry

        lax.fori_loop(first, end, one, 0)

    def contract(g):
        for j in range(4):
            g_acc[...] += lax.dot_general(
                hl[4 * g + j], t_buf[block_of(groups[g][j // 2]), 160 * (j % 2):160 * (j % 2) + 160],
                (((1,), (1,)), ((), ())), preferred_element_type=F32)

    arrive(0)
    relay(0)
    b_complete(0)
    product(0, 0, 1)
    b_arrived(1)
    b_arrived(2)
    arrive(1)
    relay(7, 1)
    b_complete(1)
    b_complete(2)
    product(0, 1, 3)
    product(1, 0, 3)
    b_arrived(3)
    b_complete(3)
    product(0, 3, 4)
    product(1, 3, 4)
    arrive(2)
    relay(6, 2)
    complete(0, 1)
    contract(0)
    product(2, 0, 4)
    complete(7, 2)
    contract(1)
    arrive(3)
    relay(5, 3)
    product(3, 0, 4)
    relay(4)
    complete(6, 3)
    contract(2)
    complete(5, 4)
    contract(3)

    row = lax.broadcasted_iota(jnp.int32, (80, 160), 0)
    col = lax.broadcasted_iota(jnp.int32, (80, 160), 1)
    diagonal = (row // 4) == (col // 8)
    left = ((lax.broadcasted_iota(jnp.int32, (8, 80), 1) % 4) == lax.broadcasted_iota(jnp.int32, (8, 80), 0)).astype(F32)
    right = ((lax.broadcasted_iota(jnp.int32, (160, 128), 0) % 8)
             == lax.broadcasted_iota(jnp.int32, (160, 128), 1)).astype(F32)
    for s in range(NX):
        both = g_acc[160 * s:160 * s + 80] + g_acc[160 * s + 80:160 * s + 160]
        both = jnp.where(diagonal, both, 0.0)
        half = jnp.dot(left, both, precision=lax.Precision.HIGHEST, preferred_element_type=F32)
        r_send[s] = jnp.dot(half, right, precision=lax.Precision.HIGHEST, preferred_element_type=F32)

    q4 = l * 2 + k
    r_copies = []
    for s in (3, 1, 2, 0):
        for e in (2, 3, 1, 0):
            if s == 0 and e == 0:
                continue
            q = (q4 + e) % 4
            copy = remote(r_send.at[s], r_in.at[4 * s + e], r_ssem.at[4 * s + e], r_rsem.at[4 * s + e],
                          dev((x + NX - SLOTS[s]) % NX, z, h, q // 2, q % 2))
            copy.start()
            r_copies.append(copy)
    total = r_send[0]
    for copy in r_copies:
        copy.wait_recv()
    for i in range(1, 16):
        total = total + r_in[i]
    out[...] = total

    for copy in r_copies:
        copy.wait_send()
    for i, copy in enumerate(a_copies):
        if i == 0:
            @pl.when(other)
            def _():
                copy.wait_send()
        else:
            copy.wait_send()
    for s in range(NX):
        f_copy(s).wait_send()
        if s:
            b_copy(s).wait_send()
    for way in range(2):
        for half in range(2):
            for step in range(last(way, half) + 1):
                za(way, half, step, sent_offset(way, step)).wait_send()

    @pl.when(t_mine)
    def _():
        for copy in t_copies:
            copy.wait_send()

    @pl.when(mine)
    def _():
        for way in range(2):
            for half in range(2):
                for step in range(last(way, half) + 1):
                    zt(way, half, step, sent_offset(way, step)).wait_send()
        for offset in range(NZ):
            to_pair(offset, l).wait_send()
            to_across(offset, l).wait_send()
            more_across(offset, 1 - l).wait_send()

    @pl.when(other)
    def _():
        for offset in range(NZ):
            more_pair(offset, 1 - l).wait_send()


def body(chol_a, chol_b, amplitudes, vir_a, vir_b, occ_pair):
    a_in = jnp.pad(chol_a.reshape(40, 1500), ((0, 0), (0, NX * PQ - 1500)))
    a_in = a_in.reshape(40, NX, PQ).transpose(1, 0, 2)
    b_in = jnp.pad(chol_b.reshape(1500, 640), ((0, NX * PQ - 1500), (0, 0)))
    t_in = amplitudes.reshape(80, 640)
    dma = pltpu.SemaphoreType.DMA
    tile = pl.pallas_call(
        kernel,
        out_shape=jax.ShapeDtypeStruct((8, 128), F32),
        in_specs=[pl.BlockSpec(memory_space=pltpu.VMEM), pl.BlockSpec(memory_space=pl.ANY),
                  pl.BlockSpec(memory_space=pltpu.VMEM)],
        out_specs=pl.BlockSpec(memory_space=pltpu.VMEM),
        scratch_shapes=[
            pltpu.VMEM((2 * NX, 40, PQ), BF16),
            pltpu.VMEM((NZ, 160, 2 * PQ), BF16),
            pltpu.VMEM((NZ, 320, 640), BF16),
            pltpu.VMEM((NX, 2 * PQ, 640), BF16),
            pltpu.VMEM((16, 640, 640), BF16),
            pltpu.VMEM((640, 160), F32),
            pltpu.VMEM((NX, 8, 128), F32),
            pltpu.VMEM((16, 8, 128), F32),
            dma((8,)), dma((8,)), dma((4,)), dma((4,)), dma((4,)), dma((4,)), dma((4,)), dma((4,)),
            dma((16,)), dma((16,)), dma((16,)), dma((16,)), dma((8,)), dma((8,)), dma((8,)), dma((8,)), dma((8,)), dma((8,)),
            dma((16,)), dma((16,)), dma((1,)),
        ],
        compiler_params=pltpu.CompilerParams(
            collective_id=0, has_side_effects=True, vmem_limit_bytes=48 * 1024 * 1024),
        cost_estimate=pl.CostEstimate(flops=7_000_000_000, bytes_accessed=16_000_000, transcendentals=0),
    )(a_in, b_in, t_in)
    pairs = occ_pair.shape[0]
    ladder = lax.dynamic_slice_in_dim(tile[:4], lax.axis_index("ch") * pairs, pairs, 1)
    energy_gap = vir_a[:, None, None] + vir_b[None, :, None] - occ_pair[None, None, :]
    return ladder[:, None, :] / energy_gap


def solution(mesh):
    return jax.shard_map(
        body,
        mesh=mesh,
        in_specs=(
            P("vp", None, "ch"),
            P("ch", "vp", None),
            P("vp", None, None),
            P(),
            P("vp"),
            P("ch"),
        ),
        out_specs=P(None, "vp", "ch"),
        check_vma=False,
    )
```

```python
import functools

import jax
import jax.numpy as jnp
from jax import lax
from jax.experimental import pallas as pl
from jax.experimental.pallas import tpu as pltpu
from jax.sharding import PartitionSpec as P

MESH = pl.DeviceIdType.MESH
NX, NZ = 4, 8
PQ = 384
WINDOW = 2
SLOTS = (0, 1, 3, 2)
BF16, F32 = jnp.bfloat16, jnp.float32


def kernel(a_hbm, b_hbm, t_hbm, va_hbm, vb_hbm, occ_hbm, out, va, vb, occ, a_raw, b_in, t_in, a_in, b_end, a_stage, a_buf, t_buf, b_buf, hl, g_acc, r_send, r_in,
           a_ssem, a_rsem, t_ssem, t_rsem, b_ssem, b_rsem, f_ssem, f_rsem,
           za_ssem, za_rsem, zt_ssem, zt_rsem, p_ssem, p_rsem, c_ssem, c_rsem, d_ssem, d_rsem,
           r_ssem, r_rsem, l_sem):
    vp, ch = lax.axis_index("vp"), lax.axis_index("ch")
    x, z, h = vp % NX, (vp // NX) % NZ, vp // (NX * NZ)
    k, l = ch % 2, ch // 2

    def dev(x_, z_, h_, l_, k_):
        return (h_ * (NX * NZ) + z_ * NX + x_, l_ * 2 + k_)

    def remote(src, dst, ssem, rsem, device):
        return pltpu.make_async_remote_copy(
            src_ref=src, dst_ref=dst, send_sem=ssem, recv_sem=rsem, device_id=device, device_id_type=MESH)

    def rows(start, size):
        return pl.ds(pl.multiple_of(start, 16), size)

    sibling = dev(x, z, h, l, 1 - k)
    above, below = dev(x, (z + 1) % NZ, h, l, k), dev(x, (z + NZ - 1) % NZ, h, l, k)
    pair = dev(x, z, h, 1 - l, k)
    across = dev(x, z, 1 - h, 1 - l, k)
    mine = k == h
    other = jnp.logical_not(mine)

    loads = [pltpu.make_async_copy(src, dst, l_sem.at[1 + i])
             for i, (src, dst) in enumerate(((a_hbm, a_raw), (t_hbm, t_in), (b_hbm, b_in)))]
    energies = [pltpu.make_async_copy(src, dst, l_sem.at[4 + i])
                for i, (src, dst) in enumerate(((va_hbm, va), (vb_hbm, vb), (occ_hbm, occ)))]
    for load in loads + energies:
        load.start()

    barrier = pltpu.get_barrier_semaphore()
    q32 = x * 8 + h * 4 + l * 2 + k

    def greet(i, carry):
        q = (q32 + i) % 32
        pl.semaphore_signal(barrier, inc=1, device_id=dev(q // 8, z, (q // 4) % 2, (q // 2) % 2, q % 2),
                            device_id_type=MESH)
        return carry

    lax.fori_loop(1, 32, greet, 0)
    pl.semaphore_signal(barrier, inc=1, device_id=above, device_id_type=MESH)
    pl.semaphore_signal(barrier, inc=1, device_id=below, device_id_type=MESH)

    for load in loads:
        load.wait()
    size = a_raw.shape[2]
    for q in range(NX):
        width = min(PQ, size - q * PQ)
        piece = a_raw[:, :, q * PQ:q * PQ + width].astype(F32)
        if width < PQ:
            piece = jnp.concatenate([piece, jnp.zeros(piece.shape[:2] + (PQ - width,), F32)], axis=2)
        a_in[q] = piece.reshape(40, PQ).astype(BF16)
    start, whole = (NX - 1) * PQ, size // 16 * 16
    b_end[0:whole - start] = b_in[start:whole]
    rest = b_in[whole:size].astype(F32)
    b_end[whole - start:PQ] = jnp.concatenate(
        [rest, jnp.zeros((NX * PQ - size, rest.shape[1]), F32)], axis=0).astype(BF16)

    pl.semaphore_wait(barrier, 33)

    t_copies = [remote(t_in, t_buf.at[z, rows(80 * x, 80)], t_ssem.at[dx], t_rsem.at[x % 2],
                       dev((x + dx) % NX, z, h, l, k)) for dx in range(1, NX)]
    t_local = pltpu.make_async_copy(t_in, t_buf.at[z, rows(80 * x, 80)], t_rsem.at[x % 2])
    t_mine = jnp.logical_and(mine, x // 2 == l)

    @pl.when(t_mine)
    def _():
        for copy in t_copies:
            copy.start()
        t_local.start()

    slot = 2 * x + k
    a_copies = []
    for dh in range(2):
        for dx in range(NX):
            to_x, to_h = (x + dx) % NX, (h + dh) % 2
            copy = remote(a_in.at[to_x], a_stage.at[slot], a_ssem.at[dh * NX + dx], a_rsem.at[slot],
                          dev(to_x, z, to_h, l, h))
            if dh == 0 and dx == 0:
                @pl.when(mine)
                def _():
                    pltpu.make_async_copy(a_in.at[x], a_stage.at[slot], a_rsem.at[slot]).start()

                @pl.when(other)
                def _():
                    copy.start()
            else:
                copy.start()
            a_copies.append(copy)

    def b_rows(core):
        return rows(core * PQ, PQ)

    def b_source(q, do):
        @pl.when(q == NX - 1)
        def _():
            do(b_end)

        @pl.when(q != NX - 1)
        def _():
            do(b_in.at[rows(jnp.minimum(q, NX - 2) * PQ, PQ)])

    def b_copy(s, src):
        return remote(src, b_buf.at[s, b_rows(k)], b_ssem.at[s], b_rsem.at[s], dev((x + SLOTS[s]) % NX, z, h, l, k))

    def f_copy(s, src=None):
        src = b_buf.at[s, b_rows(k)] if src is None else src
        return remote(src, b_buf.at[s, b_rows(k)], f_ssem.at[s], f_rsem.at[s], sibling)

    def b_stay(src):
        return pltpu.make_async_copy(src, b_buf.at[0, b_rows(k)], l_sem.at[0])

    def keep(src):
        b_stay(src).start()
        f_copy(0, src).start()

    def start_b(s):
        b_source((x + SLOTS[s]) % NX, lambda src: b_copy(s, src).start())

    start_b(1)
    start_b(2)
    b_source(x, keep)

    def last(way, half):
        return 3 if way == half else 2

    def block_of(offset):
        return (z + offset) % NZ

    def za(way, half, step, offset):
        ref = a_buf.at[block_of(offset), pl.ds(80 * half, 80)]
        i = (way * 2 + half) * 4 + step
        return remote(ref, ref, za_ssem.at[i], za_rsem.at[i], above if way == 0 else below)

    def zt(way, half, step, offset):
        ref = t_buf.at[block_of(offset), rows(160 * l + 80 * half, 80)]
        i = (way * 2 + half) * 4 + step
        return remote(ref, ref, zt_ssem.at[i], zt_rsem.at[i], above if way == 0 else below)

    def sent_offset(way, step):
        return (NZ - step) % NZ if way == 0 else step

    def got_offset(way, step):
        return NZ - 1 - step if way == 0 else 1 + step

    def quarter(offset, which, part):
        return t_buf.at[block_of(offset), rows(160 * which + 80 * part, 80)]

    def to_pair(offset, which, part):
        ref = quarter(offset, which, part)
        return remote(ref, ref, p_ssem.at[2 * offset + part], p_rsem.at[2 * offset + part], pair)

    def to_across(offset, which, part):
        ref = quarter(offset, which, part)
        return remote(ref, ref, c_ssem.at[2 * offset + part], c_rsem.at[2 * offset + part], across)

    def more_across(offset, which):
        ref = quarter(offset, which, 1)
        return remote(ref, ref, d_ssem.at[offset], d_rsem.at[offset], across)

    def more_pair(offset, which):
        ref = quarter(offset, which, 0)
        return remote(ref, ref, p_ssem.at[2 * offset], p_rsem.at[2 * offset], pair)

    def start_a():
        for origin in range(2 * NX):
            remote(a_stage.at[origin], a_stage.at[origin], a_ssem.at[0], a_rsem.at[origin], sibling).wait_recv()
        for part in range(2):
            pieces = [a_stage[2 * origin + part].astype(F32) for origin in range(NX)]
            a_buf[z, :, part * PQ:(part + 1) * PQ] = jnp.concatenate(pieces, axis=0).astype(BF16)

    def start_t():
        @pl.when(mine)
        def _():
            for half in range(2):
                ref = quarter(0, l, half)
                remote(ref, ref, t_ssem.at[0], t_rsem.at[half], sibling).wait_recv()
                for way in range(2):
                    zt(way, half, 0, 0).start()
                to_pair(0, l, half).start()
                to_across(0, l, half).start()

    g_acc[...] = jnp.zeros_like(g_acc)

    def arrive_t(step):
        @pl.when(mine)
        def _():
            for half in range(2):
                for way in range(2):
                    if step <= last(way, half):
                        offset = got_offset(way, step)
                        zt(way, half, step, offset).wait_recv()
                        if step < last(way, half):
                            zt(way, half, step + 1, offset).start()
                        to_pair(offset, l, half).start()
                        to_across(offset, l, half).start()

    flying = []

    def arrived_a(half, step):
        for way in range(2):
            if step <= last(way, half):
                za(way, half, step, got_offset(way, step)).wait_recv()

    def pass_a(half, step):
        if step > 0:
            arrived_a(half, step - 1)
        if len(flying) >= WINDOW:
            for copy in flying.pop(0):
                copy.wait_send()
        copies = [za(way, half, step, sent_offset(way, step)) for way in range(2) if step <= last(way, half)]
        for copy in copies:
            copy.start()
        flying.append(copies)

    def relay(*offsets):
        @pl.when(mine)
        def _():
            for offset in offsets:
                to_pair(offset, 1 - l, 1).wait_recv()
                more_across(offset, 1 - l).start()

        @pl.when(other)
        def _():
            for offset in offsets:
                to_across(offset, 1 - l, 0).wait_recv()
                more_pair(offset, 1 - l).start()

    def complete(*offsets):
        @pl.when(mine)
        def _():
            for offset in offsets:
                to_pair(offset, 1 - l, 0).wait_recv()

        @pl.when(other)
        def _():
            for offset in offsets:
                to_across(offset, 1 - l, 1).wait_recv()
                more_across(offset, l).wait_recv()
                more_pair(offset, l).wait_recv()

    def b_arrived(s):
        ref = b_buf.at[s, b_rows(k)]
        remote(ref, ref, b_ssem.at[s], b_rsem.at[s], sibling).wait_recv()
        f_copy(s).start()

    def b_complete(s):
        if s == 0:
            b_stay(b_end).wait()
        ref = b_buf.at[s, b_rows(1 - k)]
        remote(ref, ref, f_ssem.at[s], f_rsem.at[s], sibling).wait_recv()

    groups = ((0, 1), (7, 2), (6, 3), (5,), (4,))

    places = [[2 * (sum(len(blocks) for blocks in groups[:g]) + i) + j for i in range(len(groups[g])) for j in range(2)]
              for g in range(len(groups))]

    def product(g, first, end):
        blocks = [block_of(offset) for offset in groups[g]]

        def one(b, carry):
            left = jnp.concatenate([a_buf[block] for block in blocks], axis=0)
            v = jnp.dot(left, b_buf[b], preferred_element_type=F32)
            high = v.astype(BF16)
            low = (v - high.astype(F32)).astype(BF16)
            for j, place in enumerate(places[g]):
                hl[place, rows(b * 160, 80)] = high[80 * j:80 * j + 80]
                hl[place, rows(b * 160 + 80, 80)] = low[80 * j:80 * j + 80]
            return carry

        lax.fori_loop(first, end, one, 0)

    def contract(g):
        for j, place in enumerate(places[g]):
            g_acc[...] += lax.dot_general(
                hl[place], t_buf[block_of(groups[g][j // 2]), 160 * (j % 2):160 * (j % 2) + 160],
                (((1,), (1,)), ((), ())), preferred_element_type=F32)

    start_t()
    start_a()
    start_b(3)
    pass_a(0, 0)
    arrive_t(0)
    pass_a(1, 0)
    relay(0)
    arrive_t(1)
    pass_a(0, 1)
    relay(7, 1)
    arrive_t(2)
    pass_a(1, 1)
    b_arrived(1)
    b_arrived(2)
    b_complete(0)
    product(0, 0, 1)
    b_complete(1)
    b_complete(2)
    product(0, 1, 3)
    relay(6, 2)
    b_arrived(3)
    pass_a(0, 2)
    arrive_t(3)
    pass_a(1, 2)
    b_complete(3)
    product(0, 3, 4)
    product(1, 0, 4)
    relay(5, 3)
    pass_a(0, 3)
    pass_a(1, 3)
    complete(0, 1)
    contract(0)
    complete(7, 2)
    contract(1)
    product(2, 0, 4)
    relay(4)
    complete(6, 3)
    contract(2)
    product(3, 0, 4)
    arrived_a(0, 3)
    arrived_a(1, 3)
    product(4, 0, 4)
    complete(5, 4)
    contract(3)
    contract(4)

    row = lax.broadcasted_iota(jnp.int32, (80, 160), 0)
    col = lax.broadcasted_iota(jnp.int32, (80, 160), 1)
    diagonal = (row // 4) == (col // 8)
    left = ((lax.broadcasted_iota(jnp.int32, (8, 80), 1) % 4) == lax.broadcasted_iota(jnp.int32, (8, 80), 0)).astype(F32)
    right = ((lax.broadcasted_iota(jnp.int32, (160, 128), 0) % 8)
             == lax.broadcasted_iota(jnp.int32, (160, 128), 1)).astype(F32)
    for s in range(NX):
        both = g_acc[160 * s:160 * s + 80] + g_acc[160 * s + 80:160 * s + 160]
        both = jnp.where(diagonal, both, 0.0)
        half = jnp.dot(left, both, precision=lax.Precision.HIGHEST, preferred_element_type=F32)
        r_send[s] = jnp.dot(half, right, precision=lax.Precision.HIGHEST, preferred_element_type=F32)

    q4 = l * 2 + k
    r_copies = []
    for s in (3, 1, 2, 0):
        for e in (2, 3, 1, 0):
            if s == 0 and e == 0:
                continue
            q = (q4 + e) % 4
            copy = remote(r_send.at[s], r_in.at[4 * s + e], r_ssem.at[4 * s + e], r_rsem.at[4 * s + e],
                          dev((x + NX - SLOTS[s]) % NX, z, h, q // 2, q % 2))
            copy.start()
            r_copies.append(copy)
    for i, copy in enumerate(a_copies):
        if i == 0:
            @pl.when(other)
            def _():
                copy.wait_send()
        else:
            copy.wait_send()
    for s in range(NX):
        f_copy(s, b_end).wait_send()
        if s:
            b_copy(s, b_end).wait_send()
    for copies in flying:
        for copy in copies:
            copy.wait_send()

    @pl.when(t_mine)
    def _():
        for copy in t_copies:
            copy.wait_send()

    @pl.when(mine)
    def _():
        for way in range(2):
            for half in range(2):
                for step in range(last(way, half) + 1):
                    zt(way, half, step, sent_offset(way, step)).wait_send()
        for offset in range(NZ):
            for part in range(2):
                to_pair(offset, l, part).wait_send()
                to_across(offset, l, part).wait_send()
            more_across(offset, 1 - l).wait_send()

    @pl.when(other)
    def _():
        for offset in range(NZ):
            more_pair(offset, 1 - l).wait_send()

    total = r_send[0]
    for copy in r_copies:
        copy.wait_recv()
    for i in range(1, 16):
        total = total + r_in[i]

    for load in energies:
        load.wait()
    row = lax.broadcasted_iota(jnp.int32, (4, 2), 0)
    col = lax.broadcasted_iota(jnp.int32, (4, 2), 1)
    lane = lax.broadcasted_iota(jnp.int32, (4, 128), 1)
    ladder = [jnp.sum(jnp.where(lane == 2 * q4 + i, total[:4], 0.0), axis=1, keepdims=True) for i in range(2)]
    ladder = jnp.where(col == 0, ladder[0], ladder[1])
    first = jnp.where(row == 0, va[0], jnp.where(row == 1, va[1], jnp.where(row == 2, va[2], va[3])))
    out[...] = ladder / (first + vb[0] - jnp.where(col == 0, occ[0], occ[1]))
    for copy in r_copies:
        copy.wait_send()


def body(chol_a, chol_b, amplitudes, vir_a, vir_b, occ_pair):
    b_in = chol_b.reshape(chol_b.shape[0], chol_b.shape[2])
    t_in = amplitudes.reshape(80, 640)
    dma = pltpu.SemaphoreType.DMA
    tile = pl.pallas_call(
        kernel,
        out_shape=jax.ShapeDtypeStruct((4, 2), F32),
        in_specs=[pl.BlockSpec(memory_space=pltpu.HBM)] * 6,
        out_specs=pl.BlockSpec(memory_space=pltpu.VMEM),
        scratch_shapes=[
            pltpu.SMEM((4,), F32),
            pltpu.SMEM((1,), F32),
            pltpu.SMEM((2,), F32),
            pltpu.VMEM(chol_a.shape, BF16),
            pltpu.VMEM(b_in.shape, BF16),
            pltpu.VMEM(t_in.shape, BF16),
            pltpu.VMEM((NX, 40, PQ), BF16),
            pltpu.VMEM((PQ, 640), BF16),
            pltpu.VMEM((2 * NX, 40, PQ), BF16),
            pltpu.VMEM((NZ, 160, 2 * PQ), BF16),
            pltpu.VMEM((NZ, 320, 640), BF16),
            pltpu.VMEM((NX, 2 * PQ, 640), BF16),
            pltpu.VMEM((16, 640, 640), BF16),
            pltpu.VMEM((640, 160), F32),
            pltpu.VMEM((NX, 8, 128), F32),
            pltpu.VMEM((16, 8, 128), F32),
            dma((8,)), dma((8,)), dma((4,)), dma((4,)), dma((4,)), dma((4,)), dma((4,)), dma((4,)),
            dma((16,)), dma((16,)), dma((16,)), dma((16,)), dma((16,)), dma((16,)), dma((16,)), dma((16,)), dma((8,)), dma((8,)),
            dma((16,)), dma((16,)), dma((7,)),
        ],
        compiler_params=pltpu.CompilerParams(
            collective_id=0, has_side_effects=True, vmem_limit_bytes=64 * 1000 * 1024),
        cost_estimate=pl.CostEstimate(flops=7_000_000_000, bytes_accessed=16_000_000, transcendentals=0),
    )(chol_a, b_in, t_in, vir_a, vir_b, occ_pair)
    return tile.reshape(4, 1, 2)


def solution(mesh):
    return jax.shard_map(
        body,
        mesh=mesh,
        in_specs=(
            P("vp", None, "ch"),
            P("ch", "vp", None),
            P("vp", None, None),
            P(),
            P("vp"),
            P("ch"),
        ),
        out_specs=P(None, "vp", "ch"),
        check_vma=False,
    )
```
